32 devices in a mesh: parts: 2 (over x), rows: 16 (over z, y, core).
Axes of the slice: x: 2, y: 2, z: 4, core: 2. Of those that a mesh axis runs over, the one named last changes fastest.
Arguments:
- gain_tiles: float32 [4, 8192, 3, 128], P(None, ('parts', 'rows')), parts along dimension 1, may hold values from -0.21875 to 0.21875
- tile_pattern: int32 [8, 32, 3], P('parts'), parts along dimension 0, may hold values from 0 to 31, as said below
- offset_terms: float32 [4, 8192], P(None, ('parts', 'rows')), parts along dimension 1, may hold values from -6 to 6
- last_mean: float32 [8192], P(('parts', 'rows')), parts along dimension 0, may hold values from -6 to 6
- last_covariance: float32 [8192, 4096], P(('parts', 'rows')), parts along dimension 0, as said below
- noise_covariance: float32 [4, 8192, 4096], P(None, ('parts', 'rows')), parts along dimension 1, as said below
Outputs:
- smoothed_covariance: float32 [4, 8192, 4096], P(None, ('parts', 'rows')), parts along dimension 1
- smoothed_mean: float32 [4, 8192], P(None, ('parts', 'rows')), parts along dimension 1
The draws below stay inside these ranges and needn't reach their ends.
There are 2 independent parts, one for each index of `parts`. The reference program is written for one: setup_inputs(seed, part) draws one part's arguments, and reference() takes and returns one part's arrays. A program takes and returns all parts, laid end to end along the dimension named above; each array names one. Nothing has to cross between parts.
Inputs may be any that keep to these rules, and one draw needn't show every extreme that they name: `tile_pattern`: each tile row names 3 different tile columns; the first is the tile row's own number. `last_covariance`: symmetric. `noise_covariance`: each block's matrix is symmetric.
All inputs are finite; a program needn't handle non-finite values.
Results may differ from the reference program's by a relative error of at most 0.0001.
Values sent between devices are 32-bit elements; how exact they have to be, the bound alone decides.
A program may use at most 192 MiB of HBM per device.

```python
import math
import jax
import jax.numpy as jnp
from jax import lax

WIDTH = 4096
TILE = 128
PER_ROW = 3
BLOCKS = 4
TILE_ROWS = 32


def symmetric_draw(key, lowest, highest):
    first_key, second_key = jax.random.split(key)
    noise = jax.random.normal(first_key, (WIDTH, WIDTH), jnp.float32)
    diagonal = jnp.exp(jax.random.uniform(second_key, (WIDTH,), jnp.float32, math.log(lowest), math.log(highest)))
    return jnp.diag(diagonal) + 0.005 * 0.7071 * (noise + noise.T)


def kernel_draw(key, lowest, highest, scale_low, scale_high):
    first_key, second_key, third_key = jax.random.split(key, 3)
    noise = jax.random.normal(first_key, (WIDTH, WIDTH), jnp.float32)
    diagonal = jnp.exp(jax.random.uniform(second_key, (WIDTH,), jnp.float32, math.log(lowest), math.log(highest)))
    scales = jnp.exp(jax.random.uniform(third_key, (WIDTH,), jnp.float32, math.log(scale_low), math.log(scale_high)))
    positions = jnp.arange(WIDTH, dtype=jnp.float32)
    distance = jnp.abs(positions[:, None] - positions[None, :])
    kernel = scales[:, None] * scales[None, :] * jnp.exp(-distance / (WIDTH / 16.0))
    return jnp.diag(diagonal) + kernel + 0.02 * 0.7071 * (noise + noise.T)


def draw_last_covariance(key, part):
    return kernel_draw(jax.random.fold_in(key, 11), 0.75, 2.5, 0.5, 1.5)


def draw_noise_covariance(key, part):
    keys = jax.random.split(jax.random.fold_in(key, 23), BLOCKS)
    return jax.vmap(lambda single: symmetric_draw(single, 0.75, 2.5))(keys)


def draw_tile_pattern(key, part):
    keys = jax.random.split(jax.random.fold_in(key, 37), BLOCKS * TILE_ROWS)
    own_tiles = jnp.arange(BLOCKS * TILE_ROWS, dtype=jnp.int32) % TILE_ROWS

    def one_row(single, own_tile):
        others = jax.random.permutation(single, TILE_ROWS - 1).astype(jnp.int32) + 1
        columns = (own_tile + others[:PER_ROW - 1]) % TILE_ROWS
        return jnp.concatenate([own_tile[None], columns]).astype(jnp.int32)
    return jax.vmap(one_row)(keys, own_tiles).reshape(BLOCKS, TILE_ROWS, PER_ROW)


def shard_levels(rng, shape, pieces, least, top_value):
    level, own = 1.0, jax.random.fold_in(rng, 6)
    for axis_at, shards_of in pieces:
        draws = jnp.exp(jax.random.uniform(jax.random.fold_in(own, axis_at), (shards_of,), jnp.float32, least / len(pieces), top_value / len(pieces)))
        level = level * jnp.repeat(draws, shape[axis_at] // shards_of).reshape([-1 if axis == axis_at else 1 for axis in range(len(shape))])
    return level


def normal_values(stream_key, shape, spread, most, pieces=(), held_as=jnp.bfloat16):
    entries = jax.random.normal(stream_key, shape, jnp.float32) * spread
    if len(pieces) > 0:
        entries = shard_levels(stream_key, shape, pieces, -0.22, 0.18) * entries
    return jnp.clip(entries, min=-most, max=most).astype(held_as)


def setup_inputs(seed: int = 0, part: int = 0) -> dict:
    key_list = jax.random.split(jax.random.key(seed), 7)
    part_splits = jax.random.split(jax.random.fold_in(key_list[6], part), 7)
    gain_tiles = normal_values(part_splits[0], (BLOCKS, WIDTH, PER_ROW, TILE), (2 * PER_ROW * TILE) ** -0.5, 0.21875, ((1, 16),), jnp.float32)
    tile_pattern = draw_tile_pattern(jax.random.fold_in(jax.random.fold_in(key_list[6], part), 71), part)
    offset_terms = normal_values(part_splits[2], (BLOCKS, WIDTH), 1.0, 6.0, ((1, 16),), jnp.float32)
    last_mean = normal_values(part_splits[3], (WIDTH,), 1.0, 6.0, ((0, 16),), jnp.float32)
    last_covariance = draw_last_covariance(jax.random.fold_in(jax.random.fold_in(key_list[6], part), 71), part)
    noise_covariance = draw_noise_covariance(jax.random.fold_in(jax.random.fold_in(key_list[6], part), 71), part)
    return {"gain_tiles": gain_tiles, "tile_pattern": tile_pattern, "offset_terms": offset_terms, "last_mean": last_mean, "last_covariance": last_covariance, "noise_covariance": noise_covariance}


def right_product(dense_rows, gain_values, pattern_block):
    row_count = dense_rows.shape[0]
    tiled = dense_rows.reshape(row_count, TILE_ROWS, TILE)
    picked = tiled[:, pattern_block, :]
    shaped = gain_values.reshape(TILE_ROWS, TILE, PER_ROW, TILE)
    result = jnp.einsum("rtkj,tckj->rtc", picked, shaped, precision=lax.Precision.HIGHEST)
    return result.reshape(row_count, WIDTH)


def reference(gain_tiles, tile_pattern, offset_terms, last_mean, last_covariance, noise_covariance):
    covariance = last_covariance
    mean_vector = last_mean
    cov_list = []
    mean_list = []
    for block_index in reversed(range(BLOCKS)):
        pattern_block = tile_pattern[block_index]
        gain_values = gain_tiles[block_index]
        left_side = right_product(covariance.T, gain_values, pattern_block).T
        covariance = right_product(left_side, gain_values, pattern_block) + noise_covariance[block_index]
        mean_vector = right_product(mean_vector[None, :], gain_values, pattern_block)[0] + offset_terms[block_index]
        cov_list.append(covariance)
        mean_list.append(mean_vector)
    cov_list = cov_list[::-1]
    mean_list = mean_list[::-1]
    return jnp.stack(cov_list, 0), jnp.stack(mean_list, 0)
```

```python
import functools

import jax
import jax.numpy as jnp
from jax import lax
from jax.experimental import pallas as pl
from jax.experimental.pallas import tpu as pltpu
from jax.sharding import PartitionSpec as P

WIDTH = 4096
TILE = 128
PER_ROW = 3
BLOCKS = 4
TILE_ROWS = 32
STEP = 512
STEPS = WIDTH // STEP
PAD = 16
VMEM = 56 * 1024 * 1024


def split(x):
    high = x.astype(jnp.bfloat16)
    low = (x - high.astype(jnp.float32)).astype(jnp.bfloat16)
    return high, low


def nt(a, b):
    return lax.dot_general(a, b, (((1,), (1,)), ((), ())), preferred_element_type=jnp.float32)


def product(ah, al, bh, bl):
    return nt(ah, bh) + (nt(ah, bl) + nt(al, bh))


def gain_parts(gain_ref):
    parts = [gain_ref[:, k].reshape(STEP, TILE) for k in range(PER_ROW)]
    return split(jnp.concatenate(parts, axis=1))


def picked(ref, pattern_ref, block, tile):
    at = (block * TILE_ROWS + tile) * PER_ROW
    return jnp.concatenate([ref[pattern_ref[at + k]] for k in range(PER_ROW)], axis=1)


def right_kernel(block, pattern_ref, cov_ref, gain_ref, send_ref, high, low):
    step = pl.program_id(0)

    @pl.when(step == 0)
    def _():
        for p in range(TILE_ROWS):
            high[p], low[p] = split(cov_ref[:, p * TILE:(p + 1) * TILE])

    gh, gl = gain_parts(gain_ref)
    local = cov_ref.shape[0]
    rows = []
    for i in range(STEP // TILE):
        tile = step * (STEP // TILE) + i
        ph, pw = picked(high, pattern_ref, block, tile), picked(low, pattern_ref, block, tile)
        s = slice(i * TILE, (i + 1) * TILE)
        rows.append(product(gh[s], gl[s], ph, pw))
    send_ref[...] = jnp.concatenate(rows, axis=0).reshape(STEP // local, local, local)


def left_kernel(block, pattern_ref, recv_ref, gain_ref, noise_ref, mean_ref, offset_ref, *rest):
    cov_ref, new_mean_ref, high, low = rest[-4:]
    step = pl.program_id(0)
    local = recv_ref.shape[1]

    @pl.when(step == 0)
    def _():
        for p in range(TILE_ROWS):
            if local >= TILE:
                per = local // TILE
                x = recv_ref[p // per, :, (p % per) * TILE:(p % per + 1) * TILE]
            else:
                per = TILE // local
                x = jnp.concatenate([recv_ref[p * per + i] for i in range(per)], axis=1)
            high[p, :local], low[p, :local] = split(x)
            m = jnp.broadcast_to(mean_ref[p], (PAD, TILE))
            high[p, local:], low[p, local:] = split(m)

    gh, gl = gain_parts(gain_ref)
    for i in range(STEP // TILE):
        tile = step * (STEP // TILE) + i
        xh, xl = picked(high, pattern_ref, block, tile), picked(low, pattern_ref, block, tile)
        s = slice(i * TILE, (i + 1) * TILE)
        out = product(xh, xl, gh[s], gl[s])
        cov_ref[:, s] = out[:local] + noise_ref[:, s]
        new_mean_ref[i] = out[local:local + 1] + offset_ref[i]


def right(block, pattern, cov, cov_at, gain, n, local):
    if cov_at is None:
        cov_spec = pl.BlockSpec((local, WIDTH), lambda i, s: (0, 0))
    else:
        cov_spec = pl.BlockSpec((None, local, WIDTH), lambda i, s: (cov_at, 0, 0))
    per = STEP // local
    return pl.pallas_call(
        functools.partial(right_kernel, block),
        out_shape=jax.ShapeDtypeStruct((n, local, local), jnp.float32),
        grid_spec=pltpu.PrefetchScalarGridSpec(
            num_scalar_prefetch=1,
            grid=(STEPS,),
            in_specs=[
                cov_spec,
                pl.BlockSpec((per, PER_ROW, local, TILE), lambda i, s: (i, 0, 0, 0)),
            ],
            out_specs=pl.BlockSpec((per, local, local), lambda i, s: (i, 0, 0)),
            scratch_shapes=[pltpu.VMEM((TILE_ROWS, local, TILE), jnp.bfloat16)] * 2,
        ),
        compiler_params=pltpu.CompilerParams(vmem_limit_bytes=VMEM),
        name="right_product",
    )(pattern, cov, gain)


def left(block, pattern, recv, gain, noise, mean, offset, stack, n, local):
    per = STEP // local
    tiles = STEP // TILE
    in_specs = [
        pl.BlockSpec((n, local, local), lambda i, s: (0, 0, 0)),
        pl.BlockSpec((per, PER_ROW, local, TILE), lambda i, s: (i, 0, 0, 0)),
        pl.BlockSpec((None, local, STEP), lambda i, s: (block, 0, i)),
        pl.BlockSpec((TILE_ROWS, 1, TILE), lambda i, s: (0, 0, 0)),
        pl.BlockSpec((tiles, 1, TILE), lambda i, s: (i, 0, 0)),
    ]
    args = [pattern, recv, gain, noise, mean, offset]
    aliases = {}
    if stack is not None:
        in_specs.append(pl.BlockSpec(memory_space=pl.ANY))
        args.append(stack)
        aliases = {6: 0}
    return pl.pallas_call(
        functools.partial(left_kernel, block),
        out_shape=(
            jax.ShapeDtypeStruct((BLOCKS, local, WIDTH), jnp.float32),
            jax.ShapeDtypeStruct((TILE_ROWS, 1, TILE), jnp.float32),
        ),
        grid_spec=pltpu.PrefetchScalarGridSpec(
            num_scalar_prefetch=1,
            grid=(STEPS,),
            in_specs=in_specs,
            out_specs=(
                pl.BlockSpec((None, local, STEP), lambda i, s: (block, 0, i)),
                pl.BlockSpec((tiles, 1, TILE), lambda i, s: (i, 0, 0)),
            ),
            scratch_shapes=[pltpu.VMEM((TILE_ROWS, local + PAD, TILE), jnp.bfloat16)] * 2,
        ),
        input_output_aliases=aliases,
        compiler_params=pltpu.CompilerParams(vmem_limit_bytes=VMEM),
        name="left_product",
    )(*args)


def shards(n, gain_tiles, tile_pattern, offset_terms, last_mean, last_covariance, noise_covariance):
    local = last_mean.shape[0]
    pattern = tile_pattern.reshape(-1)
    gains = jnp.transpose(gain_tiles, (0, 2, 1, 3))
    gathered = {b: lax.all_gather(gains[b], "rows") for b in reversed(range(BLOCKS))}
    vectors = lax.all_gather(jnp.concatenate([offset_terms, last_mean[None]], 0), "rows")
    vectors = jnp.transpose(vectors, (1, 0, 2)).reshape(BLOCKS + 1, TILE_ROWS, 1, TILE)
    mean = vectors[BLOCKS]
    stack = None
    means = [None] * BLOCKS
    for b in reversed(range(BLOCKS)):
        if stack is None:
            send = right(b, pattern, last_covariance, None, gathered[b], n, local)
        else:
            send = right(b, pattern, stack, b + 1, gathered[b], n, local)
        recv = lax.all_to_all(send, "rows", split_axis=0, concat_axis=0, tiled=True)
        stack, mean = left(
            b, pattern, recv, gathered[b], noise_covariance, mean, vectors[b], stack, n, local
        )
        means[b] = mean.reshape(WIDTH)
    first = lax.axis_index("rows") * local
    own = lax.dynamic_slice(jnp.stack(means, 0), (0, first), (BLOCKS, local))
    return stack, own


def solution(mesh):
    in_specs = (
        P(None, ("parts", "rows"), None, None),
        P("parts", None, None),
        P(None, ("parts", "rows")),
        P(("parts", "rows")),
        P(("parts", "rows"), None),
        P(None, ("parts", "rows"), None),
    )
    out_specs = (P(None, ("parts", "rows"), None), P(None, ("parts", "rows")))
    return jax.shard_map(
        functools.partial(shards, mesh.shape["rows"]),
        mesh=mesh, in_specs=in_specs, out_specs=out_specs, check_vma=False,
    )
```

```python
import functools

import jax
import jax.numpy as jnp
from jax import lax
from jax.experimental import pallas as pl
from jax.experimental.pallas import tpu as pltpu
from jax.sharding import PartitionSpec as P

WIDTH = 4096
TILE = 128
PER_ROW = 3
BLOCKS = 4
TILE_ROWS = 32
STEP = 512
STEPS = WIDTH // STEP
PAD = 16
VMEM = 56 * 1024 * 1024


def split(x):
    high = x.astype(jnp.bfloat16)
    low = (x - high.astype(jnp.float32)).astype(jnp.bfloat16)
    return high, low


def nt(a, b):
    return lax.dot_general(a, b, (((1,), (1,)), ((), ())), preferred_element_type=jnp.float32)


def product(ah, al, bh, bl):
    return nt(ah, bh) + (nt(ah, bl) + nt(al, bh))


def gain_parts(gain_ref):
    cores, chips = gain_ref.shape[:2]
    rows = [
        jnp.concatenate([gain_ref[c, i, k] for k in range(PER_ROW)], axis=1)
        for i in range(chips)
        for c in range(cores)
    ]
    return split(jnp.concatenate(rows, axis=0))


def gather_gain(gain, n):
    same_core = [[2 * i + c for i in range(n // 2)] for c in range(2)]
    same_chip = [[2 * i, 2 * i + 1] for i in range(n // 2)]
    half = lax.all_gather(gain, "rows", axis_index_groups=same_core)
    return lax.all_gather(half, "rows", axis_index_groups=same_chip)


def picked(ref, pattern_ref, block, tile):
    at = (block * TILE_ROWS + tile) * PER_ROW
    return jnp.concatenate([ref[pattern_ref[at + k]] for k in range(PER_ROW)], axis=1)


def right_kernel(block, pattern_ref, cov_ref, gain_ref, send_ref, high, low):
    step = pl.program_id(0)

    @pl.when(step == 0)
    def _():
        for p in range(TILE_ROWS):
            high[p], low[p] = split(cov_ref[:, p * TILE:(p + 1) * TILE])

    gh, gl = gain_parts(gain_ref)
    local = cov_ref.shape[0]
    rows = []
    for i in range(STEP // TILE):
        tile = step * (STEP // TILE) + i
        ph, pw = picked(high, pattern_ref, block, tile), picked(low, pattern_ref, block, tile)
        s = slice(i * TILE, (i + 1) * TILE)
        rows.append(product(gh[s], gl[s], ph, pw))
    send_ref[...] = jnp.concatenate(rows, axis=0).reshape(STEP // local, local, local)


def left_kernel(block, pattern_ref, recv_ref, gain_ref, noise_ref, mean_ref, offset_ref, *rest):
    cov_ref, new_mean_ref, high, low = rest[-4:]
    step = pl.program_id(0)
    local = recv_ref.shape[1]

    @pl.when(step == 0)
    def _():
        for p in range(TILE_ROWS):
            if local >= TILE:
                per = local // TILE
                x = recv_ref[p // per, :, (p % per) * TILE:(p % per + 1) * TILE]
            else:
                per = TILE // local
                x = jnp.concatenate([recv_ref[p * per + i] for i in range(per)], axis=1)
            high[p, :local], low[p, :local] = split(x)
            m = jnp.broadcast_to(mean_ref[p], (PAD, TILE))
            high[p, local:], low[p, local:] = split(m)

    gh, gl = gain_parts(gain_ref)
    for i in range(STEP // TILE):
        tile = step * (STEP // TILE) + i
        xh, xl = picked(high, pattern_ref, block, tile), picked(low, pattern_ref, block, tile)
        s = slice(i * TILE, (i + 1) * TILE)
        out = product(xh, xl, gh[s], gl[s])
        cov_ref[:, s] = out[:local] + noise_ref[:, s]
        new_mean_ref[i] = out[local:local + 1] + offset_ref[i]


def right(block, pattern, cov, cov_at, gain, n, local):
    if cov_at is None:
        cov_spec = pl.BlockSpec((local, WIDTH), lambda i, s: (0, 0))
    else:
        cov_spec = pl.BlockSpec((None, local, WIDTH), lambda i, s: (cov_at, 0, 0))
    per = STEP // local
    return pl.pallas_call(
        functools.partial(right_kernel, block),
        out_shape=jax.ShapeDtypeStruct((n, local, local), jnp.float32),
        grid_spec=pltpu.PrefetchScalarGridSpec(
            num_scalar_prefetch=1,
            grid=(STEPS,),
            in_specs=[
                cov_spec,
                pl.BlockSpec((2, per // 2, PER_ROW, local, TILE), lambda i, s: (0, i, 0, 0, 0)),
            ],
            out_specs=pl.BlockSpec((per, local, local), lambda i, s: (i, 0, 0)),
            scratch_shapes=[pltpu.VMEM((TILE_ROWS, local, TILE), jnp.bfloat16)] * 2,
        ),
        compiler_params=pltpu.CompilerParams(vmem_limit_bytes=VMEM),
        name="right_product",
    )(pattern, cov, gain)


def left(block, pattern, recv, gain, noise, mean, offset, stack, n, local):
    per = STEP // local
    tiles = STEP // TILE
    in_specs = [
        pl.BlockSpec((n, local, local), lambda i, s: (0, 0, 0)),
        pl.BlockSpec((2, per // 2, PER_ROW, local, TILE), lambda i, s: (0, i, 0, 0, 0)),
        pl.BlockSpec((None, local, STEP), lambda i, s: (block, 0, i)),
        pl.BlockSpec((TILE_ROWS, 1, TILE), lambda i, s: (0, 0, 0)),
        pl.BlockSpec((tiles, 1, TILE), lambda i, s: (i, 0, 0)),
    ]
    args = [pattern, recv, gain, noise, mean, offset]
    aliases = {}
    if stack is not None:
        in_specs.append(pl.BlockSpec(memory_space=pl.ANY))
        args.append(stack)
        aliases = {6: 0}
    return pl.pallas_call(
        functools.partial(left_kernel, block),
        out_shape=(
            jax.ShapeDtypeStruct((BLOCKS, local, WIDTH), jnp.float32),
            jax.ShapeDtypeStruct((TILE_ROWS, 1, TILE), jnp.float32),
        ),
        grid_spec=pltpu.PrefetchScalarGridSpec(
            num_scalar_prefetch=1,
            grid=(STEPS,),
            in_specs=in_specs,
            out_specs=(
                pl.BlockSpec((None, local, STEP), lambda i, s: (block, 0, i)),
                pl.BlockSpec((tiles, 1, TILE), lambda i, s: (i, 0, 0)),
            ),
            scratch_shapes=[pltpu.VMEM((TILE_ROWS, local + PAD, TILE), jnp.bfloat16)] * 2,
        ),
        input_output_aliases=aliases,
        compiler_params=pltpu.CompilerParams(vmem_limit_bytes=VMEM),
        name="left_product",
    )(*args)


def shards(n, gain_tiles, tile_pattern, offset_terms, last_mean, last_covariance, noise_covariance):
    local = last_mean.shape[0]
    pattern = tile_pattern.reshape(-1)
    gains = jnp.transpose(gain_tiles, (0, 2, 1, 3))
    gathered = {b: gather_gain(gains[b], n) for b in reversed(range(BLOCKS))}
    vectors = lax.all_gather(jnp.concatenate([offset_terms, last_mean[None]], 0), "rows")
    vectors = jnp.transpose(vectors, (1, 0, 2)).reshape(BLOCKS + 1, TILE_ROWS, 1, TILE)
    mean = vectors[BLOCKS]
    stack = None
    means = [None] * BLOCKS
    for b in reversed(range(BLOCKS)):
        if stack is None:
            send = right(b, pattern, last_covariance, None, gathered[b], n, local)
        else:
            send = right(b, pattern, stack, b + 1, gathered[b], n, local)
        recv = lax.all_to_all(send, "rows", split_axis=0, concat_axis=0, tiled=True)
        stack, mean = left(
            b, pattern, recv, gathered[b], noise_covariance, mean, vectors[b], stack, n, local
        )
        means[b] = mean.reshape(WIDTH)
    first = lax.axis_index("rows") * local
    own = lax.dynamic_slice(jnp.stack(means, 0), (0, first), (BLOCKS, local))
    return stack, own


def solution(mesh):
    in_specs = (
        P(None, ("parts", "rows"), None, None),
        P("parts", None, None),
        P(None, ("parts", "rows")),
        P(("parts", "rows")),
        P(("parts", "rows"), None),
        P(None, ("parts", "rows"), None),
    )
    out_specs = (P(None, ("parts", "rows"), None), P(None, ("parts", "rows")))
    return jax.shard_map(
        functools.partial(shards, mesh.shape["rows"]),
        mesh=mesh, in_specs=in_specs, out_specs=out_specs, check_vma=False,
    )
```

```python
import functools

import jax
import jax.numpy as jnp
from jax import lax
from jax.experimental import pallas as pl
from jax.experimental.pallas import tpu as pltpu
from jax.sharding import PartitionSpec as P

WIDTH = 4096
TILE = 128
PER_ROW = 3
BLOCKS = 4
TILE_ROWS = 32
STEP = 512
STEPS = WIDTH // STEP
PAD = 16
VMEM = 56 * 1024 * 1024


def split(x):
    high = x.astype(jnp.bfloat16)
    low = (x - high.astype(jnp.float32)).astype(jnp.bfloat16)
    return high, low


def nt(a, b):
    return lax.dot_general(a, b, (((1,), (1,)), ((), ())), preferred_element_type=jnp.float32)


def product(ah, al, bh, bl):
    return nt(ah, bh) + (nt(ah, bl) + nt(al, bh))


def gain_parts(gain_ref):
    parts = [gain_ref[:, k].reshape(STEP, TILE) for k in range(PER_ROW)]
    return split(jnp.concatenate(parts, axis=1))


def picked(ref, pattern_ref, block, tile):
    at = (block * TILE_ROWS + tile) * PER_ROW
    return jnp.concatenate([ref[pattern_ref[at + k]] for k in range(PER_ROW)], axis=1)


def right_kernel(block, pattern_ref, cov_ref, gain_ref, send_ref, high, low):
    step = pl.program_id(0)

    @pl.when(step == 0)
    def _():
        for p in range(TILE_ROWS):
            high[p], low[p] = split(cov_ref[:, p * TILE:(p + 1) * TILE])

    gh, gl = gain_parts(gain_ref)
    local = cov_ref.shape[0]
    rows = []
    for i in range(STEP // TILE):
        tile = step * (STEP // TILE) + i
        ph, pw = picked(high, pattern_ref, block, tile), picked(low, pattern_ref, block, tile)
        s = slice(i * TILE, (i + 1) * TILE)
        rows.append(product(gh[s], gl[s], ph, pw))
    send_ref[...] = jnp.concatenate(rows, axis=0).reshape(STEP // local, local, local)


def left_kernel(block, pattern_ref, recv_ref, gain_ref, noise_ref, mean_ref, offset_ref, *rest):
    cov_ref, new_mean_ref, high, low = rest[-4:]
    step = pl.program_id(0)
    local = recv_ref.shape[1]

    @pl.when(step == 0)
    def _():
        for p in range(TILE_ROWS):
            if local >= TILE:
                per = local // TILE
                x = recv_ref[p // per, :, (p % per) * TILE:(p % per + 1) * TILE]
            else:
                per = TILE // local
                x = jnp.concatenate([recv_ref[p * per + i] for i in range(per)], axis=1)
            high[p, :local], low[p, :local] = split(x)
            m = jnp.broadcast_to(mean_ref[p], (PAD, TILE))
            high[p, local:], low[p, local:] = split(m)

    gh, gl = gain_parts(gain_ref)
    for i in range(STEP // TILE):
        tile = step * (STEP // TILE) + i
        xh, xl = picked(high, pattern_ref, block, tile), picked(low, pattern_ref, block, tile)
        s = slice(i * TILE, (i + 1) * TILE)
        out = product(xh, xl, gh[s], gl[s])
        cov_ref[:, s] = out[:local] + noise_ref[:, s]
        new_mean_ref[i] = out[local:local + 1] + offset_ref[i]


def right(block, pattern, cov, cov_at, gain, n, local):
    if cov_at is None:
        cov_spec = pl.BlockSpec((local, WIDTH), lambda i, s: (0, 0))
    else:
        cov_spec = pl.BlockSpec((None, local, WIDTH), lambda i, s: (cov_at, 0, 0))
    per = STEP // local
    return pl.pallas_call(
        functools.partial(right_kernel, block),
        out_shape=jax.ShapeDtypeStruct((n, local, local), jnp.float32),
        grid_spec=pltpu.PrefetchScalarGridSpec(
            num_scalar_prefetch=1,
            grid=(STEPS,),
            in_specs=[
                cov_spec,
                pl.BlockSpec((per, PER_ROW, local, TILE), lambda i, s: (i, 0, 0, 0)),
            ],
            out_specs=pl.BlockSpec((per, local, local), lambda i, s: (i, 0, 0)),
            scratch_shapes=[pltpu.VMEM((TILE_ROWS, local, TILE), jnp.bfloat16)] * 2,
        ),
        compiler_params=pltpu.CompilerParams(vmem_limit_bytes=VMEM),
        name="right_product",
    )(pattern, cov, gain)


def left(block, pattern, recv, gain, noise, mean, offset, stack, n, local):
    per = STEP // local
    tiles = STEP // TILE
    in_specs = [
        pl.BlockSpec((n, local, local), lambda i, s: (0, 0, 0)),
        pl.BlockSpec((per, PER_ROW, local, TILE), lambda i, s: (i, 0, 0, 0)),
        pl.BlockSpec((None, local, STEP), lambda i, s: (block, 0, i)),
        pl.BlockSpec((TILE_ROWS, 1, TILE), lambda i, s: (0, 0, 0)),
        pl.BlockSpec((tiles, 1, TILE), lambda i, s: (i, 0, 0)),
    ]
    args = [pattern, recv, gain, noise, mean, offset]
    aliases = {}
    if stack is not None:
        in_specs.append(pl.BlockSpec(memory_space=pl.ANY))
        args.append(stack)
        aliases = {6: 0}
    return pl.pallas_call(
        functools.partial(left_kernel, block),
        out_shape=(
            jax.ShapeDtypeStruct((BLOCKS, local, WIDTH), jnp.float32),
            jax.ShapeDtypeStruct((TILE_ROWS, 1, TILE), jnp.float32),
        ),
        grid_spec=pltpu.PrefetchScalarGridSpec(
            num_scalar_prefetch=1,
            grid=(STEPS,),
            in_specs=in_specs,
            out_specs=(
                pl.BlockSpec((None, local, STEP), lambda i, s: (block, 0, i)),
                pl.BlockSpec((tiles, 1, TILE), lambda i, s: (i, 0, 0)),
            ),
            scratch_shapes=[pltpu.VMEM((TILE_ROWS, local + PAD, TILE), jnp.bfloat16)] * 2,
        ),
        input_output_aliases=aliases,
        compiler_params=pltpu.CompilerParams(vmem_limit_bytes=VMEM),
        name="left_product",
    )(*args)


def shards(n, gain_tiles, tile_pattern, offset_terms, last_mean, last_covariance, noise_covariance):
    local = last_mean.shape[0]
    pattern = tile_pattern.reshape(-1)
    gains = jnp.transpose(gain_tiles, (0, 2, 1, 3))
    gathered = {BLOCKS - 1: lax.all_gather(gains[BLOCKS - 1], "rows")}
    vectors = lax.all_gather(jnp.concatenate([offset_terms, last_mean[None]], 0), "rows")
    vectors = jnp.transpose(vectors, (1, 0, 2)).reshape(BLOCKS + 1, TILE_ROWS, 1, TILE)
    mean = vectors[BLOCKS]
    stack = None
    means = [None] * BLOCKS
    for b in reversed(range(BLOCKS)):
        if stack is None:
            send = right(b, pattern, last_covariance, None, gathered[b], n, local)
        else:
            send = right(b, pattern, stack, b + 1, gathered[b], n, local)
        if b > 0:
            send, gain = lax.optimization_barrier((send, gains[b - 1]))
            gathered[b - 1] = lax.all_gather(gain, "rows")
        recv = lax.all_to_all(send, "rows", split_axis=0, concat_axis=0, tiled=True)
        stack, mean = left(
            b, pattern, recv, gathered[b], noise_covariance, mean, vectors[b], stack, n, local
        )
        means[b] = mean.reshape(WIDTH)
    first = lax.axis_index("rows") * local
    own = lax.dynamic_slice(jnp.stack(means, 0), (0, first), (BLOCKS, local))
    return stack, own


def solution(mesh):
    in_specs = (
        P(None, ("parts", "rows"), None, None),
        P("parts", None, None),
        P(None, ("parts", "rows")),
        P(("parts", "rows")),
        P(("parts", "rows"), None),
        P(None, ("parts", "rows"), None),
    )
    out_specs = (P(None, ("parts", "rows"), None), P(None, ("parts", "rows")))
    return jax.shard_map(
        functools.partial(shards, mesh.shape["rows"]),
        mesh=mesh, in_specs=in_specs, out_specs=out_specs, check_vma=False,
    )
```

```python
import functools

import jax
import jax.numpy as jnp
from jax import lax
from jax.experimental import pallas as pl
from jax.experimental.pallas import tpu as pltpu
from jax.sharding import PartitionSpec as P

WIDTH = 4096
TILE = 128
PER_ROW = 3
BLOCKS = 4
TILE_ROWS = 32
STEP = 512
STEPS = WIDTH // STEP
PAD = 16
VMEM = 56 * 1024 * 1024


def split(x):
    high = x.astype(jnp.bfloat16)
    low = (x - high.astype(jnp.float32)).astype(jnp.bfloat16)
    return high, low


def nt(a, b):
    return lax.dot_general(a, b, (((1,), (1,)), ((), ())), preferred_element_type=jnp.float32)


def product(ah, al, bh, bl):
    return nt(ah, bh) + (nt(ah, bl) + nt(al, bh))


def gain_parts(gain_ref):
    parts = [gain_ref[:, k].reshape(STEP, TILE) for k in range(PER_ROW)]
    return split(jnp.concatenate(parts, axis=1))


def picked(ref, pattern_ref, block, tile):
    at = (block * TILE_ROWS + tile) * PER_ROW
    return jnp.concatenate([ref[pattern_ref[at + k]] for k in range(PER_ROW)], axis=1)


def split_kernel(gain_ref, high_ref, low_ref):
    high_ref[...], low_ref[...] = gain_parts(gain_ref)


def split_gain(gain, local):
    shape = jax.ShapeDtypeStruct((WIDTH, PER_ROW * TILE), jnp.bfloat16)
    return pl.pallas_call(
        split_kernel,
        out_shape=(shape, shape),
        grid=(STEPS,),
        in_specs=[pl.BlockSpec((STEP // local, PER_ROW, local, TILE), lambda i: (i, 0, 0, 0))],
        out_specs=[pl.BlockSpec((STEP, PER_ROW * TILE), lambda i: (i, 0))] * 2,
        compiler_params=pltpu.CompilerParams(vmem_limit_bytes=VMEM),
        cost_estimate=pl.CostEstimate(
            flops=3 * gain.size, bytes_accessed=8 * gain.size, transcendentals=0
        ),
        name="split_gain",
    )(gain)


def right_kernel(block, pattern_ref, cov_ref, gain_ref, send_ref, high, low):
    step = pl.program_id(0)

    @pl.when(step == 0)
    def _():
        for p in range(TILE_ROWS):
            high[p], low[p] = split(cov_ref[:, p * TILE:(p + 1) * TILE])

    gh, gl = gain_parts(gain_ref)
    local = cov_ref.shape[0]
    rows = []
    for i in range(STEP // TILE):
        tile = step * (STEP // TILE) + i
        ph, pw = picked(high, pattern_ref, block, tile), picked(low, pattern_ref, block, tile)
        s = slice(i * TILE, (i + 1) * TILE)
        rows.append(product(gh[s], gl[s], ph, pw))
    send_ref[...] = jnp.concatenate(rows, axis=0).reshape(STEP // local, local, local)


def left_kernel(block, pattern_ref, recv_ref, gh_ref, gl_ref, noise_ref, mean_ref, offset_ref, *rest):
    cov_ref, new_mean_ref, high, low = rest[-4:]
    step = pl.program_id(0)
    local = recv_ref.shape[1]

    @pl.when(step == 0)
    def _():
        for p in range(TILE_ROWS):
            if local >= TILE:
                per = local // TILE
                x = recv_ref[p // per, :, (p % per) * TILE:(p % per + 1) * TILE]
            else:
                per = TILE // local
                x = jnp.concatenate([recv_ref[p * per + i] for i in range(per)], axis=1)
            high[p, :local], low[p, :local] = split(x)
            m = jnp.broadcast_to(mean_ref[p], (PAD, TILE))
            high[p, local:], low[p, local:] = split(m)

    for i in range(STEP // TILE):
        tile = step * (STEP // TILE) + i
        xh, xl = picked(high, pattern_ref, block, tile), picked(low, pattern_ref, block, tile)
        s = slice(i * TILE, (i + 1) * TILE)
        out = product(xh, xl, gh_ref[s], gl_ref[s])
        cov_ref[:, s] = out[:local] + noise_ref[:, s]
        new_mean_ref[i] = out[local:local + 1] + offset_ref[i]


def right(block, pattern, cov, cov_at, gain, n, local):
    if cov_at is None:
        cov_spec = pl.BlockSpec((local, WIDTH), lambda i, s: (0, 0))
    else:
        cov_spec = pl.BlockSpec((None, local, WIDTH), lambda i, s: (cov_at, 0, 0))
    per = STEP // local
    return pl.pallas_call(
        functools.partial(right_kernel, block),
        out_shape=jax.ShapeDtypeStruct((n, local, local), jnp.float32),
        grid_spec=pltpu.PrefetchScalarGridSpec(
            num_scalar_prefetch=1,
            grid=(STEPS,),
            in_specs=[
                cov_spec,
                pl.BlockSpec((per, PER_ROW, local, TILE), lambda i, s: (i, 0, 0, 0)),
            ],
            out_specs=pl.BlockSpec((per, local, local), lambda i, s: (i, 0, 0)),
            scratch_shapes=[pltpu.VMEM((TILE_ROWS, local, TILE), jnp.bfloat16)] * 2,
        ),
        compiler_params=pltpu.CompilerParams(vmem_limit_bytes=VMEM),
        name="right_product",
    )(pattern, cov, gain)


def left(block, pattern, recv, gain_high, gain_low, noise, mean, offset, stack, n, local):
    tiles = STEP // TILE
    in_specs = [
        pl.BlockSpec((n, local, local), lambda i, s: (0, 0, 0)),
        pl.BlockSpec((STEP, PER_ROW * TILE), lambda i, s: (i, 0)),
        pl.BlockSpec((STEP, PER_ROW * TILE), lambda i, s: (i, 0)),
        pl.BlockSpec((None, local, STEP), lambda i, s: (block, 0, i)),
        pl.BlockSpec((TILE_ROWS, 1, TILE), lambda i, s: (0, 0, 0)),
        pl.BlockSpec((tiles, 1, TILE), lambda i, s: (i, 0, 0)),
    ]
    args = [pattern, recv, gain_high, gain_low, noise, mean, offset]
    aliases = {}
    if stack is not None:
        in_specs.append(pl.BlockSpec(memory_space=pl.ANY))
        args.append(stack)
        aliases = {7: 0}
    return pl.pallas_call(
        functools.partial(left_kernel, block),
        out_shape=(
            jax.ShapeDtypeStruct((BLOCKS, local, WIDTH), jnp.float32),
            jax.ShapeDtypeStruct((TILE_ROWS, 1, TILE), jnp.float32),
        ),
        grid_spec=pltpu.PrefetchScalarGridSpec(
            num_scalar_prefetch=1,
            grid=(STEPS,),
            in_specs=in_specs,
            out_specs=(
                pl.BlockSpec((None, local, STEP), lambda i, s: (block, 0, i)),
                pl.BlockSpec((tiles, 1, TILE), lambda i, s: (i, 0, 0)),
            ),
            scratch_shapes=[pltpu.VMEM((TILE_ROWS, local + PAD, TILE), jnp.bfloat16)] * 2,
        ),
        input_output_aliases=aliases,
        compiler_params=pltpu.CompilerParams(vmem_limit_bytes=VMEM),
        name="left_product",
    )(*args)


def shards(n, gain_tiles, tile_pattern, offset_terms, last_mean, last_covariance, noise_covariance):
    local = last_mean.shape[0]
    pattern = tile_pattern.reshape(-1)
    gains = jnp.transpose(gain_tiles, (0, 2, 1, 3))
    gathered = {b: lax.all_gather(gains[b], "rows") for b in reversed(range(BLOCKS))}
    vectors = lax.all_gather(jnp.concatenate([offset_terms, last_mean[None]], 0), "rows")
    vectors = jnp.transpose(vectors, (1, 0, 2)).reshape(BLOCKS + 1, TILE_ROWS, 1, TILE)
    mean = vectors[BLOCKS]
    stack = None
    means = [None] * BLOCKS
    for b in reversed(range(BLOCKS)):
        if stack is None:
            send = right(b, pattern, last_covariance, None, gathered[b], n, local)
        else:
            send = right(b, pattern, stack, b + 1, gathered[b], n, local)
        send, gain = lax.optimization_barrier((send, gathered[b]))
        high, low = split_gain(gain, local)
        recv = lax.all_to_all(send, "rows", split_axis=0, concat_axis=0, tiled=True)
        stack, mean = left(
            b, pattern, recv, high, low, noise_covariance, mean, vectors[b], stack, n, local
        )
        means[b] = mean.reshape(WIDTH)
    first = lax.axis_index("rows") * local
    own = lax.dynamic_slice(jnp.stack(means, 0), (0, first), (BLOCKS, local))
    return stack, own


def solution(mesh):
    in_specs = (
        P(None, ("parts", "rows"), None, None),
        P("parts", None, None),
        P(None, ("parts", "rows")),
        P(("parts", "rows")),
        P(("parts", "rows"), None),
        P(None, ("parts", "rows"), None),
    )
    out_specs = (P(None, ("parts", "rows"), None), P(None, ("parts", "rows")))
    return jax.shard_map(
        functools.partial(shards, mesh.shape["rows"]),
        mesh=mesh, in_specs=in_specs, out_specs=out_specs, check_vma=False,
    )
```

```python
import functools

import jax
import jax.numpy as jnp
from jax import lax
from jax.experimental import pallas as pl
from jax.experimental.pallas import tpu as pltpu
from jax.sharding import PartitionSpec as P

WIDTH = 4096
TILE = 128
PER_ROW = 3
BLOCKS = 4
TILE_ROWS = 32
STEP = 512
STEPS = WIDTH // STEP
PAD = 16
VMEM = 56 * 1024 * 1024


def split(x):
    high = x.astype(jnp.bfloat16)
    low = (x - high.astype(jnp.float32)).astype(jnp.bfloat16)
    return high, low


def nt(a, b):
    return lax.dot_general(a, b, (((1,), (1,)), ((), ())), preferred_element_type=jnp.float32)


def product(ah, al, bh, bl):
    return nt(jnp.concatenate([ah, ah, al], axis=1), jnp.concatenate([bh, bl, bh], axis=1))


def gain_parts(gain_ref):
    parts = [gain_ref[:, k].reshape(STEP, TILE) for k in range(PER_ROW)]
    return split(jnp.concatenate(parts, axis=1))


def picked(ref, pattern_ref, block, tile):
    at = (block * TILE_ROWS + tile) * PER_ROW
    return jnp.concatenate([ref[pattern_ref[at + k]] for k in range(PER_ROW)], axis=1)


def right_kernel(block, pattern_ref, cov_ref, gain_ref, send_ref, high, low):
    step = pl.program_id(0)

    @pl.when(step == 0)
    def _():
        for p in range(TILE_ROWS):
            high[p], low[p] = split(cov_ref[:, p * TILE:(p + 1) * TILE])

    gh, gl = gain_parts(gain_ref)
    local = cov_ref.shape[0]
    rows = []
    for i in range(STEP // TILE):
        tile = step * (STEP // TILE) + i
        ph, pw = picked(high, pattern_ref, block, tile), picked(low, pattern_ref, block, tile)
        s = slice(i * TILE, (i + 1) * TILE)
        rows.append(product(gh[s], gl[s], ph, pw))
    send_ref[...] = jnp.concatenate(rows, axis=0).reshape(STEP // local, local, local)


def left_kernel(block, pattern_ref, recv_ref, gain_ref, noise_ref, mean_ref, offset_ref, *rest):
    cov_ref, new_mean_ref, high, low = rest[-4:]
    step = pl.program_id(0)
    local = recv_ref.shape[1]

    @pl.when(step == 0)
    def _():
        for p in range(TILE_ROWS):
            if local >= TILE:
                per = local // TILE
                x = recv_ref[p // per, :, (p % per) * TILE:(p % per + 1) * TILE]
            else:
                per = TILE // local
                x = jnp.concatenate([recv_ref[p * per + i] for i in range(per)], axis=1)
            high[p, :local], low[p, :local] = split(x)
            m = jnp.broadcast_to(mean_ref[p], (PAD, TILE))
            high[p, local:], low[p, local:] = split(m)

    gh, gl = gain_parts(gain_ref)
    for i in range(STEP // TILE):
        tile = step * (STEP // TILE) + i
        xh, xl = picked(high, pattern_ref, block, tile), picked(low, pattern_ref, block, tile)
        s = slice(i * TILE, (i + 1) * TILE)
        out = product(xh, xl, gh[s], gl[s])
        cov_ref[:, s] = out[:local] + noise_ref[:, s]
        new_mean_ref[i] = out[local:local + 1] + offset_ref[i]


def right(block, pattern, cov, cov_at, gain, n, local):
    if cov_at is None:
        cov_spec = pl.BlockSpec((local, WIDTH), lambda i, s: (0, 0))
    else:
        cov_spec = pl.BlockSpec((None, local, WIDTH), lambda i, s: (cov_at, 0, 0))
    per = STEP // local
    return pl.pallas_call(
        functools.partial(right_kernel, block),
        out_shape=jax.ShapeDtypeStruct((n, local, local), jnp.float32),
        grid_spec=pltpu.PrefetchScalarGridSpec(
            num_scalar_prefetch=1,
            grid=(STEPS,),
            in_specs=[
                cov_spec,
                pl.BlockSpec((per, PER_ROW, local, TILE), lambda i, s: (i, 0, 0, 0)),
            ],
            out_specs=pl.BlockSpec((per, local, local), lambda i, s: (i, 0, 0)),
            scratch_shapes=[pltpu.VMEM((TILE_ROWS, local, TILE), jnp.bfloat16)] * 2,
        ),
        compiler_params=pltpu.CompilerParams(vmem_limit_bytes=VMEM),
        name="right_product",
    )(pattern, cov, gain)


def left(block, pattern, recv, gain, noise, mean, offset, stack, n, local):
    per = STEP // local
    tiles = STEP // TILE
    in_specs = [
        pl.BlockSpec((n, local, local), lambda i, s: (0, 0, 0)),
        pl.BlockSpec((per, PER_ROW, local, TILE), lambda i, s: (i, 0, 0, 0)),
        pl.BlockSpec((None, local, STEP), lambda i, s: (block, 0, i)),
        pl.BlockSpec((TILE_ROWS, 1, TILE), lambda i, s: (0, 0, 0)),
        pl.BlockSpec((tiles, 1, TILE), lambda i, s: (i, 0, 0)),
    ]
    args = [pattern, recv, gain, noise, mean, offset]
    aliases = {}
    if stack is not None:
        in_specs.append(pl.BlockSpec(memory_space=pl.ANY))
        args.append(stack)
        aliases = {6: 0}
    return pl.pallas_call(
        functools.partial(left_kernel, block),
        out_shape=(
            jax.ShapeDtypeStruct((BLOCKS, local, WIDTH), jnp.float32),
            jax.ShapeDtypeStruct((TILE_ROWS, 1, TILE), jnp.float32),
        ),
        grid_spec=pltpu.PrefetchScalarGridSpec(
            num_scalar_prefetch=1,
            grid=(STEPS,),
            in_specs=in_specs,
            out_specs=(
                pl.BlockSpec((None, local, STEP), lambda i, s: (block, 0, i)),
                pl.BlockSpec((tiles, 1, TILE), lambda i, s: (i, 0, 0)),
            ),
            scratch_shapes=[pltpu.VMEM((TILE_ROWS, local + PAD, TILE), jnp.bfloat16)] * 2,
        ),
        input_output_aliases=aliases,
        compiler_params=pltpu.CompilerParams(vmem_limit_bytes=VMEM),
        name="left_product",
    )(*args)


def shards(n, gain_tiles, tile_pattern, offset_terms, last_mean, last_covariance, noise_covariance):
    local = last_mean.shape[0]
    pattern = tile_pattern.reshape(-1)
    gains = jnp.transpose(gain_tiles, (0, 2, 1, 3))
    gathered = {b: lax.all_gather(gains[b], "rows") for b in reversed(range(BLOCKS))}
    vectors = lax.all_gather(jnp.concatenate([offset_terms, last_mean[None]], 0), "rows")
    vectors = jnp.transpose(vectors, (1, 0, 2)).reshape(BLOCKS + 1, TILE_ROWS, 1, TILE)
    mean = vectors[BLOCKS]
    stack = None
    means = [None] * BLOCKS
    for b in reversed(range(BLOCKS)):
        if stack is None:
            send = right(b, pattern, last_covariance, None, gathered[b], n, local)
        else:
            send = right(b, pattern, stack, b + 1, gathered[b], n, local)
        recv = lax.all_to_all(send, "rows", split_axis=0, concat_axis=0, tiled=True)
        stack, mean = left(
            b, pattern, recv, gathered[b], noise_covariance, mean, vectors[b], stack, n, local
        )
        means[b] = mean.reshape(WIDTH)
    first = lax.axis_index("rows") * local
    own = lax.dynamic_slice(jnp.stack(means, 0), (0, first), (BLOCKS, local))
    return stack, own


def solution(mesh):
    in_specs = (
        P(None, ("parts", "rows"), None, None),
        P("parts", None, None),
        P(None, ("parts", "rows")),
        P(("parts", "rows")),
        P(("parts", "rows"), None),
        P(None, ("parts", "rows"), None),
    )
    out_specs = (P(None, ("parts", "rows"), None), P(None, ("parts", "rows")))
    return jax.shard_map(
        functools.partial(shards, mesh.shape["rows"]),
        mesh=mesh, in_specs=in_specs, out_specs=out_specs, check_vma=False,
    )
```
